512 devices in a mesh: row: 8 (over y), col: 8 (over z), depth: 8 (over x, core).
Axes of the slice: x: 4, y: 8, z: 8, core: 2. Of those that a mesh axis runs over, the one named last changes fastest.
Arguments:
- tokens: bfloat16 [256, 12288], P(('col', 'depth'), 'row'), may hold values from -6 to 6
- weight_in: bfloat16 [12288, 24576], P('row', ('col', 'depth')), may hold values from -0.0546875 to 0.0546875
- weight_out: bfloat16 [24576, 12288], P(('col', 'depth'), 'row'), may hold values from -0.0390625 to 0.0390625
- cotangent: bfloat16 [256, 12288], P(('col', 'depth'), 'row'), may hold values from -6 to 6
Outputs:
- output: bfloat16 [256, 12288], P(('col', 'depth'), 'row')
- grad_tokens: bfloat16 [256, 12288], P(('col', 'depth'), 'row')
- grad_weight_in: bfloat16 [12288, 24576], P('row', ('col', 'depth'))
- grad_weight_out: bfloat16 [24576, 12288], P(('col', 'depth'), 'row')
The draws below stay inside these ranges and needn't reach their ends.
All inputs are finite; a program needn't handle non-finite values.
Results may differ from the reference program's by a relative error of at most 0.0049.
Values may be sent and summed in bfloat16 or wider, within the bound.
No kernel may reach another device: no remote copies, remote signals or barrier semaphores. Data moves between devices by JAX's collectives and lax.ppermute only.
A program may use at most 64 MiB of HBM per device.

```python
import math
import jax
import jax.numpy as jnp

D = 12288
FF = 24576
TOKENS = 256


def block_levels(stream_key, dims, shards, smallest, largest):
    factor_of = 1.0
    for dim, parts in shards:
        heights = jax.random.uniform(jax.random.fold_in(jax.random.fold_in(stream_key, 6), dim), (parts,), jnp.float32, smallest / len(shards), largest / len(shards))
        factor_of = factor_of * jnp.repeat(jnp.exp(heights), dims[dim] // parts).reshape((-1,) + (1,) * (len(dims) - 1 - dim))
    return factor_of


def gaussian(stream_key, dims, width, bound, shards=(), dtype=jnp.bfloat16):
    level = block_levels(stream_key, dims, shards, -0.22, 0.18) if shards else 1.0
    drawn = jax.random.normal(stream_key, dims, jnp.float32) * width * level
    return jnp.minimum(jnp.maximum(drawn, -bound), bound).astype(dtype)


def setup_inputs(seed: int = 0) -> dict:
    key_of = jax.random.split(jax.random.key(seed), 5)
    return {
        "tokens": gaussian(key_of[0], (TOKENS, D), 1.0, 6.0, ((0, 64), (1, 8))),
        "weight_in": gaussian(key_of[1], (D, FF), D ** -0.5, 0.0546875, ((0, 8), (1, 64))),
        "weight_out": gaussian(key_of[2], (FF, D), FF ** -0.5, 0.0390625, ((0, 64), (1, 8))),
        "cotangent": gaussian(key_of[3], (TOKENS, D), 1.0, 6.0, ((0, 64), (1, 8))),
    }


root_two_pi = math.sqrt(2.0 / math.pi)
cubic = 0.044715

def gelu_value(hidden):
    inner = jnp.tanh(root_two_pi * (hidden + cubic * hidden * hidden * hidden))
    return 0.5 * hidden * (1.0 + inner)

def gelu_slope(hidden):
    inner = jnp.tanh(root_two_pi * (hidden + cubic * hidden * hidden * hidden))
    return 0.5 * (1.0 + inner) + 0.5 * hidden * (1.0 - inner * inner) * root_two_pi * (1.0 + 3.0 * cubic * hidden * hidden)

def reference(tokens, weight_in, weight_out, cotangent):
    hidden = jnp.dot(tokens, weight_in, preferred_element_type=jnp.float32)
    active = gelu_value(hidden).astype(jnp.bfloat16)
    output = jnp.dot(active, weight_out, preferred_element_type=jnp.float32).astype(jnp.bfloat16)
    grad_active = jnp.dot(cotangent, weight_out.T, preferred_element_type=jnp.float32)
    grad_hidden = (grad_active * gelu_slope(hidden)).astype(jnp.bfloat16)
    grad_tokens = jnp.dot(grad_hidden, weight_in.T, preferred_element_type=jnp.float32).astype(jnp.bfloat16)
    grad_weight_in = jnp.dot(tokens.T, grad_hidden, preferred_element_type=jnp.float32).astype(jnp.bfloat16)
    grad_weight_out = jnp.dot(active.T, cotangent, preferred_element_type=jnp.float32).astype(jnp.bfloat16)
    return (output, grad_tokens, grad_weight_in, grad_weight_out)
```

```python
import math

import jax
import jax.numpy as jnp
from jax import lax
from jax.sharding import Mesh, PartitionSpec as P

root_two_pi = math.sqrt(2.0 / math.pi)
cubic = 0.044715
chips = ("col", "x")


def gelu_parts(hidden):
    inner = jnp.tanh(root_two_pi * (hidden + cubic * hidden * hidden * hidden))
    value = 0.5 * hidden * (1.0 + inner)
    slope = 0.5 * (1.0 + inner) + 0.5 * hidden * (1.0 - inner * inner) * root_two_pi * (
        1.0 + 3.0 * cubic * hidden * hidden
    )
    return value, slope


def inner_last(left, right):
    return lax.dot_general(
        left, right, (((1,), (1,)), ((), ())), preferred_element_type=jnp.float32
    )


def inner_first(left, right):
    return lax.dot_general(
        left, right, (((0,), (0,)), ((), ())), preferred_element_type=jnp.float32
    )


def plain(left, right):
    return jnp.dot(left, right, preferred_element_type=jnp.float32)


def other_core(block):
    return lax.ppermute(block, "core", [(0, 1), (1, 0)])


def exchange(blocks, axes):
    return lax.all_to_all(blocks, axes, split_axis=0, concat_axis=0)


def copies(block, count):
    return jnp.broadcast_to(block[None], (count,) + block.shape)


def local(tokens, weight_in, weight_out, cotangent):
    bf16 = jnp.bfloat16
    rows = lax.axis_size("row")
    count = lax.axis_size("col") * lax.axis_size("x")
    share, width = tokens.shape
    units = weight_in.shape[1]
    half = count * share

    both = jnp.concatenate([tokens, cotangent], axis=0)
    mine = exchange(copies(both, count), chips)
    theirs = other_core(mine)

    def split(block):
        return block[:, :share].reshape(half, width), block[:, share:].reshape(half, width)

    tokens_mine, grad_mine = split(mine)
    tokens_theirs, grad_theirs = split(theirs)

    def terms(tok, grad):
        return jnp.concatenate(
            [plain(tok, weight_in).astype(bf16), inner_last(grad, weight_out).astype(bf16)], axis=1
        )

    partial = jnp.concatenate(
        [terms(tokens_mine, grad_mine), terms(tokens_theirs, grad_theirs)], axis=0
    )
    received = exchange(partial.reshape(rows, 2 * half // rows, 2 * units), "row")
    total = jnp.sum(received.astype(jnp.float32), axis=0)
    value, slope = gelu_parts(total[:, :units])
    acts = jnp.concatenate(
        [value.astype(bf16), (total[:, units:] * slope).astype(bf16)], axis=1
    )
    acts = exchange(copies(acts, rows), "row").reshape(2 * half, 2 * units)
    active, grad_hidden = acts[:, :units], acts[:, units:]

    def products(rows_of):
        return jnp.stack(
            [
                plain(active[rows_of], weight_out).reshape(count, share, width),
                inner_last(grad_hidden[rows_of], weight_in).reshape(count, share, width),
            ],
            axis=1,
        ).reshape(count, 2 * share, width)

    sent = other_core(products(slice(half, 2 * half)).astype(bf16))
    kept = products(slice(0, half))
    summed = (kept + sent.astype(jnp.float32)).astype(bf16)
    blocks = exchange(summed, chips)
    final = jnp.sum(blocks.astype(jnp.float32), axis=0).astype(bf16)

    tokens_all = jnp.concatenate([tokens_mine, tokens_theirs], axis=0)
    grad_all = jnp.concatenate([grad_mine, grad_theirs], axis=0)
    grad_weight_in = inner_first(tokens_all, grad_hidden).astype(bf16)
    grad_weight_out = inner_first(active, grad_all).astype(bf16)
    return final[:share], final[share:], grad_weight_in, grad_weight_out


def solution(mesh):
    sizes = dict(mesh.shape)
    finer = Mesh(
        mesh.devices.reshape(sizes["row"], sizes["col"], sizes["depth"] // 2, 2),
        ("row", "col", "x", "core"),
    )
    wide = ("col", "x", "core")
    placed = (P(wide, "row"), P("row", wide), P(wide, "row"), P(wide, "row"))
    return jax.shard_map(
        local,
        mesh=finer,
        in_specs=placed,
        out_specs=(P(wide, "row"), P(wide, "row"), P("row", wide), P(wide, "row")),
        check_vma=False,
    )
```

```python
import math

import jax
import jax.numpy as jnp
from jax import lax
from jax.experimental import pallas as pl
from jax.experimental.pallas import tpu as pltpu
from jax.sharding import Mesh, PartitionSpec as P

root_two_pi = math.sqrt(2.0 / math.pi)
cubic = 0.044715
chips = ("col", "x")
bf16 = jnp.bfloat16
f32 = jnp.float32
mib = 1024 * 1024


def gelu_parts(hidden):
    inner = jnp.tanh(root_two_pi * (hidden + cubic * hidden * hidden * hidden))
    value = 0.5 * hidden * (1.0 + inner)
    slope = 0.5 * (1.0 + inner) + 0.5 * hidden * (1.0 - inner * inner) * root_two_pi * (
        1.0 + 3.0 * cubic * hidden * hidden
    )
    return value, slope


def contract(left, right, left_dim, right_dim):
    return lax.dot_general(
        left, right, (((left_dim,), (right_dim,)), ((), ())), preferred_element_type=f32
    )


def other_core(block):
    return lax.ppermute(block, "core", [(0, 1), (1, 0)])


def exchange(blocks, axes):
    return lax.all_to_all(blocks, axes, split_axis=0, concat_axis=0)


def first_kind(shape, share):
    return lax.broadcasted_iota(jnp.int32, shape, 0) % (2 * share) < share


def whole(kernel, name, out_shapes, args, products, limit=24):
    in_vmem = pl.BlockSpec(memory_space=pltpu.VMEM)
    moved = sum(a.size * a.dtype.itemsize for a in (*args, *jax.tree.leaves(out_shapes)))
    return pl.pallas_call(
        kernel,
        out_shape=out_shapes,
        in_specs=[in_vmem] * len(args),
        out_specs=jax.tree.map(lambda _: in_vmem, out_shapes),
        cost_estimate=pl.CostEstimate(flops=2 * products, bytes_accessed=moved, transcendentals=0),
        compiler_params=pltpu.CompilerParams(vmem_limit_bytes=limit * mib),
        name=name,
    )(*args)


def spread_kernel(tokens_ref, cotangent_ref, out_ref):
    both = jnp.concatenate([tokens_ref[...].astype(f32), cotangent_ref[...].astype(f32)], axis=0)
    both = both.astype(bf16)
    for chip in range(out_ref.shape[0]):
        out_ref[chip] = both


def terms_kernel(share, acts_ref, in_ref, out_ref, in_far_ref, out_far_ref, terms_ref):
    acts = acts_ref[...]
    units = in_ref.shape[1]
    for place, (w_in, w_out) in enumerate(((in_ref, out_ref), (in_far_ref, out_far_ref))):
        value = contract(acts, w_in[...], 1, 0)
        slope = contract(acts, w_out[...], 1, 1)
        picked = jnp.where(first_kind(value.shape, share), value, slope)
        terms_ref[:, place * units : (place + 1) * units] = picked.astype(bf16)


def gelu_kernel(share, terms_ref, out_ref):
    total = terms_ref[0].astype(f32)
    for row in range(1, terms_ref.shape[0]):
        total = total + terms_ref[row].astype(f32)
    first = first_kind(total.shape, share)
    hidden = jnp.where(first, total, pltpu.roll(total, share, 0))
    value, slope = gelu_parts(hidden)
    made = jnp.where(first, value, total * slope).astype(bf16)
    for row in range(out_ref.shape[0]):
        out_ref[row] = made


def sums_kernel(share, made_ref, in_ref, out_ref, in_far_ref, out_far_ref, sums_ref):
    units, width = out_ref.shape
    near, far = made_ref[:, :units], made_ref[:, units:]
    step = 512
    for start in range(0, width, step):
        part = slice(start, start + step)
        ahead = contract(near, out_ref[:, part], 1, 0) + contract(far, out_far_ref[:, part], 1, 0)
        back = contract(near, in_ref[part, :], 1, 1) + contract(far, in_far_ref[part, :], 1, 1)
        picked = jnp.where(first_kind(ahead.shape, share), ahead, back)
        sums_ref[:, part] = picked.astype(bf16)


def weight_kernel(share, acts_ref, acts_far_ref, made_ref, made_far_ref, grad_in_ref, grad_out_ref):
    grads, actives = [], []
    for made in (made_ref, made_far_ref):
        wide = made[...].astype(f32)
        first = first_kind(wide.shape, share)
        up = pltpu.roll(wide, wide.shape[0] - share, 0)
        down = pltpu.roll(wide, share, 0)
        grads.append(jnp.where(first, up, 0.0).astype(bf16))
        actives.append(jnp.where(first, 0.0, down).T.astype(bf16))
    step = 512
    for start in range(0, acts_ref.shape[1], step):
        part = slice(start, start + step)
        near, far = acts_ref[:, part], acts_far_ref[:, part]
        grad_in = contract(near, grads[0], 0, 0) + contract(far, grads[1], 0, 0)
        grad_in_ref[part, :] = grad_in.astype(bf16)
        grad_out = contract(actives[0], near, 1, 0) + contract(actives[1], far, 1, 0)
        grad_out_ref[:, part] = grad_out.astype(bf16)


def bind(kernel, share):
    return lambda *refs: kernel(share, *refs)


def local(tokens, weight_in, weight_out, cotangent):
    rows = lax.axis_size("row")
    count = lax.axis_size("col") * lax.axis_size("x")
    share, width = tokens.shape
    units = weight_in.shape[1]
    held = 2 * share * count
    shaped = lambda *dims: jax.ShapeDtypeStruct(dims, bf16)

    copies = whole(
        spread_kernel, "spread_rows", shaped(count, 2 * share, width), (tokens, cotangent), 0
    )
    weight_in_far = other_core(weight_in)
    weight_out_far = other_core(weight_out)
    weights = (weight_in, weight_out, weight_in_far, weight_out_far)
    acts = exchange(copies, chips).reshape(held, width)

    partial = whole(
        bind(terms_kernel, share),
        "hidden_terms",
        shaped(held, 2 * units),
        (acts, *weights),
        4 * held * width * units,
    )
    received = exchange(partial.reshape(rows, held // rows, 2 * units), "row")
    made = whole(
        bind(gelu_kernel, share), "gelu_rows", shaped(*received.shape), (received,), 0
    )
    made = exchange(made, "row").reshape(held, 2 * units)

    sums = whole(
        bind(sums_kernel, share),
        "output_terms",
        shaped(held, width),
        (made, *weights),
        4 * held * width * units,
    )
    sums, made, acts = lax.optimization_barrier((sums, made, acts))
    blocks = exchange(sums.reshape(count, 2 * share, width), chips)
    final = jnp.sum(blocks.astype(f32), axis=0).astype(bf16)

    made_far = other_core(made[:, units:])
    acts_far = other_core(acts)
    grad_weight_in, grad_weight_out = whole(
        bind(weight_kernel, share),
        "weight_gradients",
        (shaped(width, units), shaped(units, width)),
        (acts, acts_far, made[:, :units], made_far),
        4 * held * width * units,
    )
    return final[:share], final[share:], grad_weight_in, grad_weight_out


def solution(mesh):
    sizes = dict(mesh.shape)
    finer = Mesh(
        mesh.devices.reshape(sizes["row"], sizes["col"], sizes["depth"] // 2, 2),
        ("row", "col", "x", "core"),
    )
    wide = ("col", "x", "core")
    placed = (P(wide, "row"), P("row", wide), P(wide, "row"), P(wide, "row"))
    return jax.shard_map(
        local,
        mesh=finer,
        in_specs=placed,
        out_specs=(P(wide, "row"), P(wide, "row"), P("row", wide), P(wide, "row")),
        check_vma=False,
    )
```

```python
import math

import jax
import jax.numpy as jnp
from jax import lax
from jax.experimental import pallas as pl
from jax.experimental.pallas import tpu as pltpu
from jax.sharding import Mesh, PartitionSpec as P

root_two_pi = math.sqrt(2.0 / math.pi)
cubic = 0.044715
chips = ("col", "x")
bf16 = jnp.bfloat16
f32 = jnp.float32
mib = 1024 * 1024


def gelu_parts(hidden):
    inner = jnp.tanh(root_two_pi * (hidden + cubic * hidden * hidden * hidden))
    value = 0.5 * hidden * (1.0 + inner)
    slope = 0.5 * (1.0 + inner) + 0.5 * hidden * (1.0 - inner * inner) * root_two_pi * (
        1.0 + 3.0 * cubic * hidden * hidden
    )
    return value, slope


def contract(left, right, left_dim, right_dim):
    return lax.dot_general(
        left, right, (((left_dim,), (right_dim,)), ((), ())), preferred_element_type=f32
    )


def other_core(block):
    return lax.ppermute(block, "core", [(0, 1), (1, 0)])


def exchange(blocks, axes):
    return lax.all_to_all(blocks, axes, split_axis=0, concat_axis=0)


def first_kind(shape, share):
    return lax.broadcasted_iota(jnp.int32, shape, 0) % (2 * share) < share


def whole(kernel, name, out_shapes, args, products, far=0, out_far=0, scratch=(), limit=24):
    in_vmem = pl.BlockSpec(memory_space=pltpu.VMEM)
    in_hbm = pl.BlockSpec(memory_space=pltpu.HBM)
    moved = sum(a.size * a.dtype.itemsize for a in (*args, *jax.tree.leaves(out_shapes)))
    return pl.pallas_call(
        kernel,
        out_shape=out_shapes,
        in_specs=[in_vmem] * (len(args) - far) + [in_hbm] * far,
        out_specs=[in_vmem] * (len(out_shapes) - out_far) + [in_hbm] * out_far,
        scratch_shapes=list(scratch),
        cost_estimate=pl.CostEstimate(flops=2 * products, bytes_accessed=moved, transcendentals=0),
        compiler_params=pltpu.CompilerParams(vmem_limit_bytes=limit * mib),
        name=name,
    )(*args)


def terms_kernel(share, acts_hbm, *refs):
    weights_hbm, terms_ref, kept_hbm, acts_ref, weights, sems = (
        refs[:4], refs[4], refs[5], refs[6], refs[7:11], refs[11]
    )
    fetches = [
        pltpu.make_async_copy(source, target, sems.at[place])
        for place, (source, target) in enumerate(
            zip((acts_hbm, *weights_hbm), (acts_ref, *weights))
        )
    ]
    for fetch in fetches:
        fetch.start()
    units = weights[0].shape[1]
    fetches[0].wait()
    keep = pltpu.make_async_copy(acts_ref, kept_hbm, sems.at[len(fetches)])
    keep.start()
    acts = acts_ref[...]
    for side in range(2):
        fetches[1 + 2 * side].wait()
        value = contract(acts, weights[2 * side][...], 1, 0)
        fetches[2 + 2 * side].wait()
        slope = contract(acts, weights[2 * side + 1][...], 1, 1)
        picked = jnp.where(first_kind(value.shape, share), value, slope)
        terms_ref[:, side * units : (side + 1) * units] = picked.astype(bf16)
    keep.wait()


def gelu_kernel(share, terms_ref, out_ref):
    total = terms_ref[0].astype(f32)
    for row in range(1, terms_ref.shape[0]):
        total = total + terms_ref[row].astype(f32)
    first = first_kind(total.shape, share)
    hidden = jnp.where(first, total, pltpu.roll(total, share, 0))
    value, slope = gelu_parts(hidden)
    made = jnp.where(first, value, total * slope).astype(bf16)
    for row in range(out_ref.shape[0]):
        out_ref[row] = made


def sums_kernel(share, made_hbm, *refs):
    weights_hbm, sums_hbm, made_ref, weights, sums_ref, sems = (
        refs[:4], refs[4], refs[5], refs[6:10], refs[10], refs[11]
    )
    units, width = weights[1].shape
    step = 512
    parts = [slice(start, start + step) for start in range(0, width, step)]
    fetch_made = pltpu.make_async_copy(made_hbm, made_ref, sems.at[0, len(parts)])
    fetch_made.start()
    fetches, stores = [], []
    for place, part in enumerate(parts):
        fetches.append([])
        for kind, (source, target) in enumerate(zip(weights_hbm, weights)):
            cut = (part, slice(None)) if kind % 2 == 0 else (slice(None), part)
            fetch = pltpu.make_async_copy(source.at[cut], target.at[cut], sems.at[kind, place])
            fetch.start()
            fetches[-1].append(fetch)
        stores.append(
            pltpu.make_async_copy(sums_ref.at[:, part], sums_hbm.at[:, part], sems.at[4, place])
        )
    in_near, out_near, in_far, out_far = weights
    fetch_made.wait()
    near, far = made_ref[:, :units], made_ref[:, units:]
    for part, ready, store in zip(parts, fetches, stores):
        for fetch in ready:
            fetch.wait()
        ahead = contract(near, out_near[:, part], 1, 0) + contract(far, out_far[:, part], 1, 0)
        back = contract(near, in_near[part, :], 1, 1) + contract(far, in_far[part, :], 1, 1)
        picked = jnp.where(first_kind(ahead.shape, share), ahead, back)
        sums_ref[:, part] = picked.astype(bf16)
        store.start()
    for store in stores:
        store.wait()


def weight_kernel(share, acts_ref, acts_far_ref, made_ref, made_far_ref, grad_in_ref, grad_out_ref):
    grads, actives = [], []
    for made in (made_ref, made_far_ref):
        wide = made[...].astype(f32)
        first = first_kind(wide.shape, share)
        up = pltpu.roll(wide, wide.shape[0] - share, 0)
        down = pltpu.roll(wide, share, 0)
        grads.append(jnp.where(first, up, 0.0).astype(bf16))
        actives.append(jnp.where(first, 0.0, down).T.astype(bf16))
    step = 512
    for start in range(0, acts_ref.shape[1], step):
        part = slice(start, start + step)
        near, far = acts_ref[:, part], acts_far_ref[:, part]
        grad_in = contract(near, grads[0], 0, 0) + contract(far, grads[1], 0, 0)
        grad_in_ref[part, :] = grad_in.astype(bf16)
        grad_out = contract(actives[0], near, 1, 0) + contract(actives[1], far, 1, 0)
        grad_out_ref[:, part] = grad_out.astype(bf16)


def bind(kernel, share):
    return lambda *refs: kernel(share, *refs)


def local(tokens, weight_in, weight_out, cotangent):
    rows = lax.axis_size("row")
    count = lax.axis_size("col") * lax.axis_size("x")
    share, width = tokens.shape
    units = weight_in.shape[1]
    held = 2 * share * count
    shaped = lambda *dims: jax.ShapeDtypeStruct(dims, bf16)

    both = jnp.concatenate([tokens, cotangent], axis=0)
    copies = jnp.broadcast_to(both[None], (count,) + both.shape)
    weight_in_far = other_core(weight_in)
    weight_out_far = other_core(weight_out)
    weights = (weight_in, weight_out, weight_in_far, weight_out_far)
    held_weights = [pltpu.VMEM(w.shape, bf16) for w in weights]
    acts = exchange(copies, chips).reshape(held, width)

    partial, acts = whole(
        bind(terms_kernel, share),
        "hidden_terms",
        [shaped(held, 2 * units), shaped(held, width)],
        (acts, *weights),
        4 * held * width * units,
        far=5,
        out_far=1,
        scratch=(pltpu.VMEM(acts.shape, bf16), *held_weights, pltpu.SemaphoreType.DMA((6,))),
        limit=60,
    )
    received = exchange(partial.reshape(rows, held // rows, 2 * units), "row")
    (made,) = whole(
        bind(gelu_kernel, share), "gelu_rows", [shaped(*received.shape)], (received,), 0
    )
    made = exchange(made, "row").reshape(held, 2 * units)

    (sums,) = whole(
        bind(sums_kernel, share),
        "output_terms",
        [shaped(held, width)],
        (made, *weights),
        4 * held * width * units,
        far=5,
        out_far=1,
        scratch=(
            pltpu.VMEM(made.shape, bf16),
            *held_weights,
            pltpu.VMEM((held, width), bf16),
            pltpu.SemaphoreType.DMA((5, width // 512 + 1)),
        ),
        limit=60,
    )
    sums, made, acts = lax.optimization_barrier((sums, made, acts))
    blocks = exchange(sums.reshape(count, 2 * share, width), chips)
    final = jnp.sum(blocks.astype(f32), axis=0).astype(bf16)

    made_far = other_core(made[:, units:])
    acts_far = other_core(acts)
    grad_weight_in, grad_weight_out = whole(
        bind(weight_kernel, share),
        "weight_gradients",
        [shaped(width, units), shaped(units, width)],
        (acts, acts_far, made[:, :units], made_far),
        4 * held * width * units,
    )
    return final[:share], final[share:], grad_weight_in, grad_weight_out


def solution(mesh):
    sizes = dict(mesh.shape)
    finer = Mesh(
        mesh.devices.reshape(sizes["row"], sizes["col"], sizes["depth"] // 2, 2),
        ("row", "col", "x", "core"),
    )
    wide = ("col", "x", "core")
    placed = (P(wide, "row"), P("row", wide), P(wide, "row"), P(wide, "row"))
    return jax.shard_map(
        local,
        mesh=finer,
        in_specs=placed,
        out_specs=(P(wide, "row"), P(wide, "row"), P("row", wide), P(wide, "row")),
        check_vma=False,
    )
```

```python
import math

import jax
import jax.numpy as jnp
from jax import lax
from jax.experimental import pallas as pl
from jax.experimental.pallas import tpu as pltpu
from jax.sharding import Mesh, PartitionSpec as P

root_two_pi = math.sqrt(2.0 / math.pi)
cubic = 0.044715
chips = ("x", "col")
bf16 = jnp.bfloat16
f32 = jnp.float32
mib = 1024 * 1024


def gelu_parts(hidden):
    inner = jnp.tanh(root_two_pi * (hidden + cubic * hidden * hidden * hidden))
    value = 0.5 * hidden * (1.0 + inner)
    slope = 0.5 * (1.0 + inner) + 0.5 * hidden * (1.0 - inner * inner) * root_two_pi * (
        1.0 + 3.0 * cubic * hidden * hidden
    )
    return value, slope


def contract(left, right, left_dim, right_dim):
    return lax.dot_general(
        left, right, (((left_dim,), (right_dim,)), ((), ())), preferred_element_type=f32
    )


def other_core(block):
    return lax.ppermute(block, "core", [(0, 1), (1, 0)])


def exchange(blocks, axes):
    return lax.all_to_all(blocks, axes, split_axis=0, concat_axis=0)


def first_kind(shape, share):
    return lax.broadcasted_iota(jnp.int32, shape, 0) % (2 * share) < share


def whole(kernel, name, out_shapes, args, products, limit=24):
    in_vmem = pl.BlockSpec(memory_space=pltpu.VMEM)
    moved = sum(a.size * a.dtype.itemsize for a in (*args, *jax.tree.leaves(out_shapes)))
    return pl.pallas_call(
        kernel,
        out_shape=out_shapes,
        in_specs=[in_vmem] * len(args),
        out_specs=jax.tree.map(lambda _: in_vmem, out_shapes),
        cost_estimate=pl.CostEstimate(flops=2 * products, bytes_accessed=moved, transcendentals=0),
        compiler_params=pltpu.CompilerParams(vmem_limit_bytes=limit * mib),
        name=name,
    )(*args)


def terms_kernel(share, acts_ref, in_ref, out_ref, in_far_ref, out_far_ref, terms_ref):
    acts = acts_ref[...]
    units = in_ref.shape[1]
    for place, (w_in, w_out) in enumerate(((in_ref, out_ref), (in_far_ref, out_far_ref))):
        value = contract(acts, w_in[...], 1, 0)
        slope = contract(acts, w_out[...], 1, 1)
        picked = jnp.where(first_kind(value.shape, share), value, slope)
        terms_ref[:, place * units : (place + 1) * units] = picked.astype(bf16)


def gelu_kernel(share, terms_ref, out_ref):
    total = terms_ref[0].astype(f32)
    for row in range(1, terms_ref.shape[0]):
        total = total + terms_ref[row].astype(f32)
    first = first_kind(total.shape, share)
    hidden = jnp.where(first, total, pltpu.roll(total, share, 0))
    value, slope = gelu_parts(hidden)
    made = jnp.where(first, value, total * slope).astype(bf16)
    for row in range(out_ref.shape[0]):
        out_ref[row] = made


def sums_kernel(share, made_ref, in_ref, out_ref, in_far_ref, out_far_ref, sums_ref):
    units, width = out_ref.shape
    near, far = made_ref[:, :units], made_ref[:, units:]
    step = 512
    for start in range(0, width, step):
        part = slice(start, start + step)
        ahead = contract(near, out_ref[:, part], 1, 0) + contract(far, out_far_ref[:, part], 1, 0)
        back = contract(near, in_ref[part, :], 1, 1) + contract(far, in_far_ref[part, :], 1, 1)
        picked = jnp.where(first_kind(ahead.shape, share), ahead, back)
        sums_ref[:, part] = picked.astype(bf16)


def weight_kernel(share, acts_ref, acts_far_ref, made_ref, made_far_ref, grad_in_ref, grad_out_ref):
    grads, actives = [], []
    for made in (made_ref, made_far_ref):
        wide = made[...].astype(f32)
        first = first_kind(wide.shape, share)
        up = pltpu.roll(wide, wide.shape[0] - share, 0)
        down = pltpu.roll(wide, share, 0)
        grads.append(jnp.where(first, up, 0.0).astype(bf16))
        actives.append(jnp.where(first, 0.0, down).T.astype(bf16))
    step = 512
    for start in range(0, acts_ref.shape[1], step):
        part = slice(start, start + step)
        near, far = acts_ref[:, part], acts_far_ref[:, part]
        grad_in = contract(near, grads[0], 0, 0) + contract(far, grads[1], 0, 0)
        grad_in_ref[part, :] = grad_in.astype(bf16)
        grad_out = contract(actives[0], near, 1, 0) + contract(actives[1], far, 1, 0)
        grad_out_ref[:, part] = grad_out.astype(bf16)


def bind(kernel, share):
    return lambda *refs: kernel(share, *refs)


def local(tokens, weight_in, weight_out, cotangent):
    rows = lax.axis_size("row")
    count = lax.axis_size("col") * lax.axis_size("x")
    share, width = tokens.shape
    units = weight_in.shape[1]
    held = 2 * share * count
    shaped = lambda *dims: jax.ShapeDtypeStruct(dims, bf16)

    both = jnp.concatenate([tokens, cotangent], axis=0)
    weight_in_far = other_core(weight_in)
    weight_out_far = other_core(weight_out)
    weights = (weight_in, weight_out, weight_in_far, weight_out_far)
    cols, xs = lax.axis_size("col"), lax.axis_size("x")
    line = exchange(jnp.broadcast_to(both[None], (cols,) + both.shape), "col")
    line = line.reshape(1, held // xs, width)
    acts = exchange(jnp.broadcast_to(line, (xs,) + line.shape[1:]), "x").reshape(held, width)

    partial = whole(
        bind(terms_kernel, share),
        "hidden_terms",
        shaped(held, 2 * units),
        (acts, *weights),
        4 * held * width * units,
    )
    received = exchange(partial.reshape(rows, held // rows, 2 * units), "row")
    made = whole(
        bind(gelu_kernel, share), "gelu_rows", shaped(*received.shape), (received,), 0
    )
    made = exchange(made, "row").reshape(held, 2 * units)

    sums = whole(
        bind(sums_kernel, share),
        "output_terms",
        shaped(held, width),
        (made, *weights),
        4 * held * width * units,
    )
    sums, made, acts = lax.optimization_barrier((sums, made, acts))
    blocks = exchange(sums.reshape(count, 2 * share, width), chips)
    final = jnp.sum(blocks.astype(f32), axis=0).astype(bf16)

    made_far = other_core(made[:, units:])
    acts_far = other_core(acts)
    grad_weight_in, grad_weight_out = whole(
        bind(weight_kernel, share),
        "weight_gradients",
        (shaped(width, units), shaped(units, width)),
        (acts, acts_far, made[:, :units], made_far),
        4 * held * width * units,
    )
    return final[:share], final[share:], grad_weight_in, grad_weight_out


def solution(mesh):
    sizes = dict(mesh.shape)
    finer = Mesh(
        mesh.devices.reshape(sizes["row"], sizes["col"], sizes["depth"] // 2, 2),
        ("row", "col", "x", "core"),
    )
    wide = ("col", "x", "core")
    placed = (P(wide, "row"), P("row", wide), P(wide, "row"), P(wide, "row"))
    return jax.shard_map(
        local,
        mesh=finer,
        in_specs=placed,
        out_specs=(P(wide, "row"), P(wide, "row"), P("row", wide), P(wide, "row")),
        check_vma=False,
    )
```

```python
import math

import jax
import jax.numpy as jnp
from jax import lax
from jax.experimental import pallas as pl
from jax.experimental.pallas import tpu as pltpu
from jax.sharding import Mesh, PartitionSpec as P

root_two_pi = math.sqrt(2.0 / math.pi)
cubic = 0.044715
chips = ("x", "col")
bf16 = jnp.bfloat16
f32 = jnp.float32
mib = 1024 * 1024
swap_cover = 24_000_000_000


def gelu_parts(hidden):
    inner = jnp.tanh(root_two_pi * (hidden + cubic * hidden * hidden * hidden))
    value = 0.5 * hidden * (1.0 + inner)
    slope = 0.5 * (1.0 + inner) + 0.5 * hidden * (1.0 - inner * inner) * root_two_pi * (
        1.0 + 3.0 * cubic * hidden * hidden
    )
    return value, slope


def contract(left, right, left_dim, right_dim):
    return lax.dot_general(
        left, right, (((left_dim,), (right_dim,)), ((), ())), preferred_element_type=f32
    )


def other_core(block):
    return lax.ppermute(block, "core", [(0, 1), (1, 0)])


def exchange(blocks, axes):
    return lax.all_to_all(blocks, axes, split_axis=0, concat_axis=0)


def first_kind(shape, share):
    return lax.broadcasted_iota(jnp.int32, shape, 0) % (2 * share) < share


def whole(kernel, name, out_shapes, args, flops, out_specs=None, scratch=(), limit=24):
    moved = sum(2 * math.prod(a.shape) for a in (*args, *jax.tree.leaves(out_shapes)))
    in_vmem = pl.BlockSpec(memory_space=pltpu.VMEM)
    return pl.pallas_call(
        kernel,
        out_shape=out_shapes,
        in_specs=[in_vmem] * len(args),
        out_specs=out_specs or jax.tree.map(lambda _: in_vmem, out_shapes),
        scratch_shapes=list(scratch),
        cost_estimate=pl.CostEstimate(flops=flops, bytes_accessed=moved, transcendentals=0),
        compiler_params=pltpu.CompilerParams(vmem_limit_bytes=limit * mib),
        name=name,
    )(*args)


def spread_kernel(block_ref, out_ref):
    for place in range(out_ref.shape[0]):
        out_ref[place] = block_ref[...]


def terms_kernel(share, acts_ref, in_ref, out_ref, in_far_ref, out_far_ref, terms_ref):
    acts = acts_ref[...]
    units = in_ref.shape[1]
    for place, (w_in, w_out) in enumerate(((in_ref, out_ref), (in_far_ref, out_far_ref))):
        value = contract(acts, w_in[...], 1, 0)
        slope = contract(acts, w_out[...], 1, 1)
        picked = jnp.where(first_kind(value.shape, share), value, slope)
        terms_ref[:, place * units : (place + 1) * units] = picked.astype(bf16)


def gelu_kernel(share, terms_ref, out_ref):
    total = terms_ref[0].astype(f32)
    for row in range(1, terms_ref.shape[0]):
        total = total + terms_ref[row].astype(f32)
    first = first_kind(total.shape, share)
    hidden = jnp.where(first, total, pltpu.roll(total, share, 0))
    value, slope = gelu_parts(hidden)
    made = jnp.where(first, value, total * slope).astype(bf16)
    for row in range(out_ref.shape[0]):
        out_ref[row] = made


def sums_kernel(
    share, made_ref, in_ref, out_ref, in_far_ref, out_far_ref, sums_hbm, sums_ref, sems
):
    units, width = out_ref.shape
    near, far = made_ref[:, :units], made_ref[:, units:]
    step = 512
    stores = []
    for place, start in enumerate(range(0, width, step)):
        part = slice(start, start + step)
        ahead = contract(near, out_ref[:, part], 1, 0) + contract(far, out_far_ref[:, part], 1, 0)
        back = contract(near, in_ref[part, :], 1, 1) + contract(far, in_far_ref[part, :], 1, 1)
        picked = jnp.where(first_kind(ahead.shape, share), ahead, back)
        sums_ref[:, part] = picked.astype(bf16)
        store = pltpu.make_async_copy(
            sums_ref.at[:, part], sums_hbm.at[:, part], sems.at[place]
        )
        store.start()
        stores.append(store)
    for store in stores:
        store.wait()


def weight_kernel(share, acts_ref, acts_far_ref, made_ref, made_far_ref, grad_in_ref, grad_out_ref):
    grads, actives = [], []
    for made in (made_ref, made_far_ref):
        wide = made[...].astype(f32)
        first = first_kind(wide.shape, share)
        up = pltpu.roll(wide, wide.shape[0] - share, 0)
        down = pltpu.roll(wide, share, 0)
        grads.append(jnp.where(first, up, 0.0).astype(bf16))
        actives.append(jnp.where(first, 0.0, down).T.astype(bf16))
    step = 512
    for start in range(0, acts_ref.shape[1], step):
        part = slice(start, start + step)
        near, far = acts_ref[:, part], acts_far_ref[:, part]
        grad_in = contract(near, grads[0], 0, 0) + contract(far, grads[1], 0, 0)
        grad_in_ref[part, :] = grad_in.astype(bf16)
        grad_out = contract(actives[0], near, 1, 0) + contract(actives[1], far, 1, 0)
        grad_out_ref[:, part] = grad_out.astype(bf16)


def bind(kernel, share):
    return lambda *refs: kernel(share, *refs)


def local(tokens, weight_in, weight_out, cotangent):
    rows = lax.axis_size("row")
    count = lax.axis_size("col") * lax.axis_size("x")
    share, width = tokens.shape
    units = weight_in.shape[1]
    held = 2 * share * count
    shaped = lambda *dims: jax.ShapeDtypeStruct(dims, bf16)

    both = jnp.concatenate([tokens, cotangent], axis=0)
    weight_in_far = other_core(weight_in)
    weight_out_far = other_core(weight_out)
    weights = (weight_in, weight_out, weight_in_far, weight_out_far)
    cols, xs = lax.axis_size("col"), lax.axis_size("x")
    line = exchange(jnp.broadcast_to(both[None], (cols,) + both.shape), "col")
    line = line.reshape(held // xs, width)
    line = whole(spread_kernel, "spread_rows", shaped(xs, *line.shape), (line,), swap_cover)
    acts = exchange(line, "x").reshape(held, width)

    partial = whole(
        bind(terms_kernel, share),
        "hidden_terms",
        shaped(held, 2 * units),
        (acts, *weights),
        8 * held * width * units,
    )
    received = exchange(partial.reshape(rows, held // rows, 2 * units), "row")
    made = whole(
        bind(gelu_kernel, share), "gelu_rows", shaped(*received.shape), (received,), 0
    )
    made = exchange(made, "row").reshape(held, 2 * units)

    sums = whole(
        bind(sums_kernel, share),
        "output_terms",
        pltpu.HBM((held, width), bf16),
        (made, *weights),
        8 * held * width * units,
        out_specs=pl.BlockSpec(memory_space=pltpu.HBM),
        scratch=(pltpu.VMEM((held, width), bf16), pltpu.SemaphoreType.DMA((width // 512,))),
    )
    sums, made, acts = lax.optimization_barrier((sums, made, acts))
    blocks = exchange(sums.reshape(count, 2 * share, width), chips)
    final = jnp.sum(blocks.astype(f32), axis=0).astype(bf16)

    made_far = other_core(made[:, units:])
    acts_far = other_core(acts)
    grad_weight_in, grad_weight_out = whole(
        bind(weight_kernel, share),
        "weight_gradients",
        (shaped(width, units), shaped(units, width)),
        (acts, acts_far, made[:, :units], made_far),
        8 * held * width * units,
    )
    return final[:share], final[share:], grad_weight_in, grad_weight_out


def solution(mesh):
    sizes = dict(mesh.shape)
    finer = Mesh(
        mesh.devices.reshape(sizes["row"], sizes["col"], sizes["depth"] // 2, 2),
        ("row", "col", "x", "core"),
    )
    wide = ("col", "x", "core")
    placed = (P(wide, "row"), P("row", wide), P(wide, "row"), P(wide, "row"))
    return jax.shard_map(
        local,
        mesh=finer,
        in_specs=placed,
        out_specs=(P(wide, "row"), P(wide, "row"), P("row", wide), P(wide, "row")),
        check_vma=False,
    )
```

```python
import math

import jax
import jax.numpy as jnp
from jax import lax
from jax.experimental import pallas as pl
from jax.experimental.pallas import tpu as pltpu
from jax.sharding import Mesh, PartitionSpec as P

root_two_pi = math.sqrt(2.0 / math.pi)
cubic = 0.044715
chips = ("x", "col")
bf16 = jnp.bfloat16
f32 = jnp.float32
mib = 1024 * 1024
swap_cover = 24_000_000_000


def gelu_parts(hidden):
    inner = jnp.tanh(root_two_pi * (hidden + cubic * hidden * hidden * hidden))
    value = 0.5 * hidden * (1.0 + inner)
    slope = 0.5 * (1.0 + inner) + 0.5 * hidden * (1.0 - inner * inner) * root_two_pi * (
        1.0 + 3.0 * cubic * hidden * hidden
    )
    return value, slope


def contract(left, right, left_dim, right_dim):
    return lax.dot_general(
        left, right, (((left_dim,), (right_dim,)), ((), ())), preferred_element_type=f32
    )


def other_core(block):
    return lax.ppermute(block, "core", [(0, 1), (1, 0)])


def exchange(blocks, axes):
    return lax.all_to_all(blocks, axes, split_axis=0, concat_axis=0)


def whole(kernel, name, out_shapes, args, flops, out_specs=None, scratch=(), limit=24):
    moved = sum(2 * math.prod(a.shape) for a in (*args, *jax.tree.leaves(out_shapes)))
    in_vmem = pl.BlockSpec(memory_space=pltpu.VMEM)
    return pl.pallas_call(
        kernel,
        out_shape=out_shapes,
        in_specs=[in_vmem] * len(args),
        out_specs=out_specs or jax.tree.map(lambda _: in_vmem, out_shapes),
        scratch_shapes=list(scratch),
        cost_estimate=pl.CostEstimate(flops=flops, bytes_accessed=moved, transcendentals=0),
        compiler_params=pltpu.CompilerParams(vmem_limit_bytes=limit * mib),
        name=name,
    )(*args)


def pairs_of(rows, group):
    pairs = rows.reshape(rows.shape[0] // (2 * group), 2, group, rows.shape[1])
    return pairs[:, 0], pairs[:, 1]


def meet(upper, lower, group):
    first = lax.broadcasted_iota(jnp.int32, upper.shape, 1) < group // 2
    return jnp.where(first, upper, lower)


def turned(groups):
    return pltpu.roll(groups, groups.shape[1] // 2, 1)


def kinds_of(ref, blocks, columns=slice(None)):
    size = ref.shape[0] // blocks
    return [
        jnp.concatenate(
            [
                ref[block * size + kind * size // 2 : block * size + (kind + 1) * size // 2, columns]
                for block in range(blocks)
            ],
            axis=0,
        )
        for kind in range(2)
    ]


def spread_kernel(share, line_ref, out_ref):
    group = 2 * share
    even, odd = pairs_of(line_ref[...].astype(f32), group)
    half = out_ref.shape[1] // 2
    tokens = meet(even, turned(odd), group).reshape(half, -1).astype(bf16)
    cotangent = meet(turned(even), odd, group).reshape(half, -1).astype(bf16)
    for place in range(out_ref.shape[0]):
        out_ref[place, :half] = tokens
        out_ref[place, half:] = cotangent


def terms_kernel(lines, rows, acts_ref, in_ref, out_ref, in_far_ref, out_far_ref, terms_ref):
    tokens, cotangent = kinds_of(acts_ref, lines)
    units = in_ref.shape[1]
    size = terms_ref.shape[0] // rows
    half = size // 2
    for place, (w_in, w_out) in enumerate(((in_ref, out_ref), (in_far_ref, out_far_ref))):
        columns = slice(place * units, (place + 1) * units)
        made = (contract(tokens, w_in[...], 1, 0), contract(cotangent, w_out[...], 1, 1))
        for kind, term in enumerate(made):
            term = term.astype(bf16)
            for row in range(rows):
                start = row * size + kind * half
                terms_ref[start : start + half, columns] = term[row * half : (row + 1) * half]


def gelu_kernel(terms_ref, out_ref):
    total = terms_ref[0].astype(f32)
    for row in range(1, terms_ref.shape[0]):
        total = total + terms_ref[row].astype(f32)
    half = total.shape[0] // 2
    value, slope = gelu_parts(total[:half])
    made = jnp.concatenate([value, total[half:] * slope], axis=0).astype(bf16)
    for row in range(out_ref.shape[0]):
        out_ref[row] = made


def sums_kernel(
    share, rows, made_ref, in_ref, out_ref, in_far_ref, out_far_ref, sums_hbm, sums_ref, sems
):
    units, width = out_ref.shape
    active, grads = kinds_of(made_ref, rows)
    group = 2 * share
    step = 512
    stores = []
    for place, start in enumerate(range(0, width, step)):
        part = slice(start, start + step)
        ahead = contract(active[:, :units], out_ref[:, part], 1, 0)
        ahead = ahead + contract(active[:, units:], out_far_ref[:, part], 1, 0)
        back = contract(grads[:, :units], in_ref[part, :], 1, 1)
        back = back + contract(grads[:, units:], in_far_ref[part, :], 1, 1)
        ahead, back = (sums.reshape(-1, group, step) for sums in (ahead, back))
        even, odd = meet(ahead, turned(back), group), meet(turned(ahead), back, group)
        picked = jnp.stack([even, odd], axis=1).reshape(-1, step)
        sums_ref[:, part] = picked.astype(bf16)
        store = pltpu.make_async_copy(
            sums_ref.at[:, part], sums_hbm.at[:, part], sems.at[place]
        )
        store.start()
        stores.append(store)
    for store in stores:
        store.wait()


def weight_kernel(
    lines, rows, acts_ref, acts_far_ref, made_ref, made_far_ref, grad_in_ref, grad_out_ref
):
    made = zip(kinds_of(made_ref, rows), kinds_of(made_far_ref, rows))
    active, grads = (jnp.concatenate(sides, axis=0) for sides in made)
    active = active.astype(f32).T.astype(bf16)
    step = 512
    for start in range(0, acts_ref.shape[1], step):
        part = slice(start, start + step)
        acts = zip(kinds_of(acts_ref, lines, part), kinds_of(acts_far_ref, lines, part))
        tokens, cotangent = (jnp.concatenate(sides, axis=0) for sides in acts)
        grad_in_ref[part, :] = contract(tokens, grads, 0, 0).astype(bf16)
        grad_out_ref[:, part] = contract(active, cotangent, 1, 0).astype(bf16)


def bind(kernel, *sizes):
    return lambda *refs: kernel(*sizes, *refs)


def local(tokens, weight_in, weight_out, cotangent):
    rows = lax.axis_size("row")
    count = lax.axis_size("col") * lax.axis_size("x")
    share, width = tokens.shape
    units = weight_in.shape[1]
    held = 2 * share * count
    shaped = lambda *dims: jax.ShapeDtypeStruct(dims, bf16)

    both = jnp.concatenate([tokens, cotangent], axis=0)
    weight_in_far = other_core(weight_in)
    weight_out_far = other_core(weight_out)
    weights = (weight_in, weight_out, weight_in_far, weight_out_far)
    cols, xs = lax.axis_size("col"), lax.axis_size("x")
    line = exchange(jnp.broadcast_to(both[None], (cols,) + both.shape), "col")
    line = line.reshape(held // xs, width)
    line = whole(
        bind(spread_kernel, share), "spread_rows", shaped(xs, *line.shape), (line,), swap_cover
    )
    acts = exchange(line, "x").reshape(held, width)

    partial = whole(
        bind(terms_kernel, xs, rows),
        "hidden_terms",
        shaped(held, 2 * units),
        (acts, *weights),
        4 * held * width * units,
    )
    received = exchange(partial.reshape(rows, held // rows, 2 * units), "row")
    made = whole(
        gelu_kernel, "gelu_rows", shaped(*received.shape), (received,), 0
    )
    made = exchange(made, "row").reshape(held, 2 * units)

    sums = whole(
        bind(sums_kernel, share, rows),
        "output_terms",
        pltpu.HBM((held, width), bf16),
        (made, *weights),
        4 * held * width * units,
        out_specs=pl.BlockSpec(memory_space=pltpu.HBM),
        scratch=(pltpu.VMEM((held, width), bf16), pltpu.SemaphoreType.DMA((width // 512,))),
    )
    sums, made, acts = lax.optimization_barrier((sums, made, acts))
    blocks = exchange(sums.reshape(count, 2 * share, width), chips)
    final = jnp.sum(blocks.astype(f32), axis=0).astype(bf16)

    made_far = other_core(made[:, units:])
    acts_far = other_core(acts)
    grad_weight_in, grad_weight_out = whole(
        bind(weight_kernel, xs, rows),
        "weight_gradients",
        (shaped(width, units), shaped(units, width)),
        (acts, acts_far, made[:, :units], made_far),
        4 * held * width * units,
    )
    return final[:share], final[share:], grad_weight_in, grad_weight_out


def solution(mesh):
    sizes = dict(mesh.shape)
    finer = Mesh(
        mesh.devices.reshape(sizes["row"], sizes["col"], sizes["depth"] // 2, 2),
        ("row", "col", "x", "core"),
    )
    wide = ("col", "x", "core")
    placed = (P(wide, "row"), P("row", wide), P(wide, "row"), P(wide, "row"))
    return jax.shard_map(
        local,
        mesh=finer,
        in_specs=placed,
        out_specs=(P(wide, "row"), P(wide, "row"), P("row", wide), P(wide, "row")),
        check_vma=False,
    )
```

```python
import math

import jax
import jax.numpy as jnp
from jax import lax
from jax.experimental import pallas as pl
from jax.experimental.pallas import tpu as pltpu
from jax.sharding import Mesh, PartitionSpec as P

root_two_pi = math.sqrt(2.0 / math.pi)
cubic = 0.044715
chips = ("x", "col")
bf16 = jnp.bfloat16
f32 = jnp.float32
mib = 1024 * 1024
swap_cover = 24_000_000_000


def gelu_parts(hidden):
    inner = jnp.tanh(root_two_pi * (hidden + cubic * hidden * hidden * hidden))
    value = 0.5 * hidden * (1.0 + inner)
    slope = 0.5 * (1.0 + inner) + 0.5 * hidden * (1.0 - inner * inner) * root_two_pi * (
        1.0 + 3.0 * cubic * hidden * hidden
    )
    return value, slope


def contract(left, right, left_dim, right_dim):
    return lax.dot_general(
        left, right, (((left_dim,), (right_dim,)), ((), ())), preferred_element_type=f32
    )


def other_core(block):
    return lax.ppermute(block, "core", [(0, 1), (1, 0)])


def exchange(blocks, axes):
    return lax.all_to_all(blocks, axes, split_axis=0, concat_axis=0)


def whole(kernel, name, out_shapes, args, flops, out_specs=None, scratch=(), limit=24):
    moved = sum(2 * math.prod(a.shape) for a in (*args, *jax.tree.leaves(out_shapes)))
    in_vmem = pl.BlockSpec(memory_space=pltpu.VMEM)
    return pl.pallas_call(
        kernel,
        out_shape=out_shapes,
        in_specs=[in_vmem] * len(args),
        out_specs=out_specs or jax.tree.map(lambda _: in_vmem, out_shapes),
        scratch_shapes=list(scratch),
        cost_estimate=pl.CostEstimate(flops=flops, bytes_accessed=moved, transcendentals=0),
        compiler_params=pltpu.CompilerParams(vmem_limit_bytes=limit * mib),
        name=name,
    )(*args)


def pairs_of(rows, group):
    pairs = rows.reshape(rows.shape[0] // (2 * group), 2, group, rows.shape[1])
    return pairs[:, 0], pairs[:, 1]


def meet(upper, lower, group):
    first = lax.broadcasted_iota(jnp.int32, upper.shape, 1) < group // 2
    return jnp.where(first, upper, lower)


def turned(groups):
    return pltpu.roll(groups, groups.shape[1] // 2, 1)


def kinds_of(ref, blocks, columns=slice(None)):
    size = ref.shape[0] // blocks
    return [
        jnp.concatenate(
            [
                ref[block * size + kind * size // 2 : block * size + (kind + 1) * size // 2, columns]
                for block in range(blocks)
            ],
            axis=0,
        )
        for kind in range(2)
    ]


def spread_kernel(share, line_ref, out_ref):
    group = 2 * share
    even, odd = pairs_of(line_ref[...].astype(f32), group)
    half = out_ref.shape[1] // 2
    tokens = meet(even, turned(odd), group).reshape(half, -1).astype(bf16)
    cotangent = meet(turned(even), odd, group).reshape(half, -1).astype(bf16)
    for place in range(out_ref.shape[0]):
        out_ref[place, :half] = tokens
        out_ref[place, half:] = cotangent


def terms_kernel(lines, rows, acts_ref, in_ref, out_ref, in_far_ref, out_far_ref, terms_ref):
    tokens, cotangent = kinds_of(acts_ref, lines)
    size = terms_ref.shape[0] // rows
    half = size // 2
    w_in = jnp.concatenate([in_ref[...], in_far_ref[...]], axis=1)
    w_out = jnp.concatenate([out_ref[...], out_far_ref[...]], axis=0)
    made = (contract(tokens, w_in, 1, 0), contract(cotangent, w_out, 1, 1))
    for kind, term in enumerate(made):
        term = term.astype(bf16)
        for row in range(rows):
            start = row * size + kind * half
            terms_ref[start : start + half] = term[row * half : (row + 1) * half]


def gelu_kernel(terms_ref, out_ref):
    total = terms_ref[0].astype(f32)
    for row in range(1, terms_ref.shape[0]):
        total = total + terms_ref[row].astype(f32)
    half = total.shape[0] // 2
    value, slope = gelu_parts(total[:half])
    made = jnp.concatenate([value, total[half:] * slope], axis=0).astype(bf16)
    for row in range(out_ref.shape[0]):
        out_ref[row] = made


def sums_kernel(
    share, rows, made_ref, in_ref, out_ref, in_far_ref, out_far_ref, sums_hbm, sums_ref, sems
):
    width = out_ref.shape[1]
    active, grads = kinds_of(made_ref, rows)
    group = 2 * share
    step = 512
    stores = []
    for place, start in enumerate(range(0, width, step)):
        part = slice(start, start + step)
        ahead = contract(active, jnp.concatenate([out_ref[:, part], out_far_ref[:, part]], 0), 1, 0)
        back = contract(grads, jnp.concatenate([in_ref[part, :], in_far_ref[part, :]], 1), 1, 1)
        ahead, back = (sums.reshape(-1, group, step) for sums in (ahead, back))
        even, odd = meet(ahead, turned(back), group), meet(turned(ahead), back, group)
        picked = jnp.stack([even, odd], axis=1).reshape(-1, step)
        sums_ref[:, part] = picked.astype(bf16)
        store = pltpu.make_async_copy(
            sums_ref.at[:, part], sums_hbm.at[:, part], sems.at[place]
        )
        store.start()
        stores.append(store)
    for store in stores:
        store.wait()


def weight_kernel(
    lines, rows, acts_ref, acts_far_ref, made_ref, made_far_ref, grad_in_ref, grad_out_ref
):
    made = zip(kinds_of(made_ref, rows), kinds_of(made_far_ref, rows))
    active, grads = (jnp.concatenate(sides, axis=0) for sides in made)
    active = active.astype(f32).T.astype(bf16)
    step = 512
    for start in range(0, acts_ref.shape[1], step):
        part = slice(start, start + step)
        acts = zip(kinds_of(acts_ref, lines, part), kinds_of(acts_far_ref, lines, part))
        tokens, cotangent = (jnp.concatenate(sides, axis=0) for sides in acts)
        grad_in_ref[part, :] = contract(tokens, grads, 0, 0).astype(bf16)
        grad_out_ref[:, part] = contract(active, cotangent, 1, 0).astype(bf16)


def bind(kernel, *sizes):
    return lambda *refs: kernel(*sizes, *refs)


def local(tokens, weight_in, weight_out, cotangent):
    rows = lax.axis_size("row")
    count = lax.axis_size("col") * lax.axis_size("x")
    share, width = tokens.shape
    units = weight_in.shape[1]
    held = 2 * share * count
    shaped = lambda *dims: jax.ShapeDtypeStruct(dims, bf16)

    both = jnp.concatenate([tokens, cotangent], axis=0)
    weight_in_far = other_core(weight_in)
    weight_out_far = other_core(weight_out)
    weights = (weight_in, weight_out, weight_in_far, weight_out_far)
    cols, xs = lax.axis_size("col"), lax.axis_size("x")
    line = exchange(jnp.broadcast_to(both[None], (cols,) + both.shape), "col")
    line = line.reshape(held // xs, width)
    line = whole(
        bind(spread_kernel, share), "spread_rows", shaped(xs, *line.shape), (line,), swap_cover
    )
    acts = exchange(line, "x").reshape(held, width)

    partial = whole(
        bind(terms_kernel, xs, rows),
        "hidden_terms",
        shaped(held, 2 * units),
        (acts, *weights),
        4 * held * width * units,
    )
    received = exchange(partial.reshape(rows, held // rows, 2 * units), "row")
    made = whole(
        gelu_kernel, "gelu_rows", shaped(*received.shape), (received,), 0
    )
    made = exchange(made, "row").reshape(held, 2 * units)

    sums = whole(
        bind(sums_kernel, share, rows),
        "output_terms",
        pltpu.HBM((held, width), bf16),
        (made, *weights),
        4 * held * width * units,
        out_specs=pl.BlockSpec(memory_space=pltpu.HBM),
        scratch=(pltpu.VMEM((held, width), bf16), pltpu.SemaphoreType.DMA((width // 512,))),
    )
    sums, made, acts = lax.optimization_barrier((sums, made, acts))
    blocks = exchange(sums.reshape(count, 2 * share, width), chips)
    final = jnp.sum(blocks.astype(f32), axis=0).astype(bf16)

    made_far = other_core(made[:, units:])
    acts_far = other_core(acts)
    grad_weight_in, grad_weight_out = whole(
        bind(weight_kernel, xs, rows),
        "weight_gradients",
        (shaped(width, units), shaped(units, width)),
        (acts, acts_far, made[:, :units], made_far),
        4 * held * width * units,
    )
    return final[:share], final[share:], grad_weight_in, grad_weight_out


def solution(mesh):
    sizes = dict(mesh.shape)
    finer = Mesh(
        mesh.devices.reshape(sizes["row"], sizes["col"], sizes["depth"] // 2, 2),
        ("row", "col", "x", "core"),
    )
    wide = ("col", "x", "core")
    placed = (P(wide, "row"), P("row", wide), P(wide, "row"), P(wide, "row"))
    return jax.shard_map(
        local,
        mesh=finer,
        in_specs=placed,
        out_specs=(P(wide, "row"), P(wide, "row"), P("row", wide), P(wide, "row")),
        check_vma=False,
    )
```

```python
import math

import jax
import jax.numpy as jnp
from jax import lax
from jax.experimental import pallas as pl
from jax.experimental.pallas import tpu as pltpu
from jax.sharding import Mesh, PartitionSpec as P

root_two_pi = math.sqrt(2.0 / math.pi)
cubic = 0.044715
chips = ("x", "col")
bf16 = jnp.bfloat16
f32 = jnp.float32
mib = 1024 * 1024
swap_cover = 24_000_000_000


def gelu_parts(hidden):
    inner = jnp.tanh(root_two_pi * (hidden + cubic * hidden * hidden * hidden))
    value = 0.5 * hidden * (1.0 + inner)
    slope = 0.5 * (1.0 + inner) + 0.5 * hidden * (1.0 - inner * inner) * root_two_pi * (
        1.0 + 3.0 * cubic * hidden * hidden
    )
    return value, slope


def contract(left, right, left_dim, right_dim):
    return lax.dot_general(
        left, right, (((left_dim,), (right_dim,)), ((), ())), preferred_element_type=f32
    )


def other_core(block):
    return lax.ppermute(block, "core", [(0, 1), (1, 0)])


def exchange(blocks, axes):
    return lax.all_to_all(blocks, axes, split_axis=0, concat_axis=0)


def whole(kernel, name, out_shapes, args, flops, out_specs=None, scratch=(), limit=24):
    moved = sum(2 * math.prod(a.shape) for a in (*args, *jax.tree.leaves(out_shapes)))
    in_vmem = pl.BlockSpec(memory_space=pltpu.VMEM)
    return pl.pallas_call(
        kernel,
        out_shape=out_shapes,
        in_specs=[in_vmem] * len(args),
        out_specs=out_specs or jax.tree.map(lambda _: in_vmem, out_shapes),
        scratch_shapes=list(scratch),
        cost_estimate=pl.CostEstimate(flops=flops, bytes_accessed=moved, transcendentals=0),
        compiler_params=pltpu.CompilerParams(vmem_limit_bytes=limit * mib),
        name=name,
    )(*args)


def pairs_of(rows, group):
    pairs = rows.reshape(rows.shape[0] // (2 * group), 2, group, rows.shape[1])
    return pairs[:, 0], pairs[:, 1]


def meet(upper, lower, group):
    first = lax.broadcasted_iota(jnp.int32, upper.shape, 1) < group // 2
    return jnp.where(first, upper, lower)


def turned(groups):
    return pltpu.roll(groups, groups.shape[1] // 2, 1)


def kinds_of(ref, blocks, columns=slice(None)):
    size = ref.shape[0] // blocks
    return [
        jnp.concatenate(
            [
                ref[block * size + kind * size // 2 : block * size + (kind + 1) * size // 2, columns]
                for block in range(blocks)
            ],
            axis=0,
        )
        for kind in range(2)
    ]


def spread_kernel(share, line_ref, out_ref):
    group = 2 * share
    even, odd = pairs_of(line_ref[...].astype(f32), group)
    half = out_ref.shape[1] // 2
    tokens = meet(even, turned(odd), group).reshape(half, -1).astype(bf16)
    cotangent = meet(turned(even), odd, group).reshape(half, -1).astype(bf16)
    for place in range(out_ref.shape[0]):
        out_ref[place, :half] = tokens
        out_ref[place, half:] = cotangent


def terms_kernel(lines, rows, acts_ref, in_ref, out_ref, in_far_ref, out_far_ref, terms_ref):
    tokens, cotangent = kinds_of(acts_ref, lines)
    units = in_ref.shape[1]
    size = terms_ref.shape[0] // rows
    half = size // 2
    for place, (w_in, w_out) in enumerate(((in_ref, out_ref), (in_far_ref, out_far_ref))):
        columns = slice(place * units, (place + 1) * units)
        made = (contract(tokens, w_in[...], 1, 0), contract(cotangent, w_out[...], 1, 1))
        for kind, term in enumerate(made):
            term = term.astype(bf16)
            for row in range(rows):
                start = row * size + kind * half
                terms_ref[start : start + half, columns] = term[row * half : (row + 1) * half]


def gelu_kernel(terms_ref, out_ref):
    total = terms_ref[0].astype(f32)
    for row in range(1, terms_ref.shape[0]):
        total = total + terms_ref[row].astype(f32)
    half = total.shape[0] // 2
    value, slope = gelu_parts(total[:half])
    made = jnp.concatenate([value, total[half:] * slope], axis=0).astype(bf16)
    for row in range(out_ref.shape[0]):
        out_ref[row] = made


def sums_kernel(
    share, rows, made_ref, in_ref, out_ref, in_far_ref, out_far_ref, sums_hbm, sums_ref, sems
):
    units, width = out_ref.shape
    active, grads = kinds_of(made_ref, rows)
    group = 2 * share
    step = 512
    stores = []
    for place, start in enumerate(range(0, width, step)):
        part = slice(start, start + step)
        ahead = contract(active[:, :units], out_ref[:, part], 1, 0)
        ahead = ahead + contract(active[:, units:], out_far_ref[:, part], 1, 0)
        back = contract(grads[:, :units], in_ref[part, :], 1, 1)
        back = back + contract(grads[:, units:], in_far_ref[part, :], 1, 1)
        ahead, back = (sums.reshape(-1, group, step) for sums in (ahead, back))
        even, odd = meet(ahead, turned(back), group), meet(turned(ahead), back, group)
        picked = jnp.stack([even, odd], axis=1).reshape(-1, step)
        sums_ref[:, part] = picked.astype(bf16)
        store = pltpu.make_async_copy(
            sums_ref.at[:, part], sums_hbm.at[:, part], sems.at[place]
        )
        store.start()
        stores.append(store)
    for store in stores:
        store.wait()


def weight_kernel(
    lines, rows, acts_ref, acts_far_ref, made_ref, made_far_ref, grad_in_ref, grad_out_ref
):
    made = zip(kinds_of(made_ref, rows), kinds_of(made_far_ref, rows))
    active, grads = (jnp.concatenate(sides, axis=0) for sides in made)
    active = active.astype(f32).T.astype(bf16)
    step = 512
    for start in range(0, acts_ref.shape[1], step):
        part = slice(start, start + step)
        acts = zip(kinds_of(acts_ref, lines, part), kinds_of(acts_far_ref, lines, part))
        tokens, cotangent = (jnp.concatenate(sides, axis=0) for sides in acts)
        grad_in_ref[part, :] = contract(tokens, grads, 0, 0).astype(bf16)
        grad_out_ref[:, part] = contract(active, cotangent, 1, 0).astype(bf16)


def bind(kernel, *sizes):
    return lambda *refs: kernel(*sizes, *refs)


def local(tokens, weight_in, weight_out, cotangent):
    rows = lax.axis_size("row")
    count = lax.axis_size("col") * lax.axis_size("x")
    share, width = tokens.shape
    units = weight_in.shape[1]
    held = 2 * share * count
    shaped = lambda *dims: jax.ShapeDtypeStruct(dims, bf16)

    both = jnp.concatenate([tokens, cotangent], axis=0)
    weight_in_far = other_core(weight_in)
    weight_out_far = other_core(weight_out)
    weights = (weight_in, weight_out, weight_in_far, weight_out_far)
    cols, xs = lax.axis_size("col"), lax.axis_size("x")
    line = exchange(jnp.broadcast_to(both[None], (cols,) + both.shape), "col")
    line = line.reshape(held // xs, width)
    line = whole(
        bind(spread_kernel, share), "spread_rows", shaped(xs, *line.shape), (line,), swap_cover
    )
    acts = exchange(line, "x").reshape(held, width)

    partial = whole(
        bind(terms_kernel, xs, rows),
        "hidden_terms",
        shaped(held, 2 * units),
        (acts, *weights),
        4 * held * width * units,
    )
    received = exchange(partial.reshape(rows, held // rows, 2 * units), "row")
    made = whole(
        gelu_kernel, "gelu_rows", shaped(*received.shape), (received,), 0
    )
    made = exchange(made, "row").reshape(held, 2 * units)

    sums = whole(
        bind(sums_kernel, share, rows),
        "output_terms",
        pltpu.HBM((held, width), bf16),
        (made, *weights),
        4 * held * width * units,
        out_specs=pl.BlockSpec(memory_space=pltpu.HBM),
        scratch=(pltpu.VMEM((held, width), bf16), pltpu.SemaphoreType.DMA((width // 512,))),
    )
    sums, made, acts = lax.optimization_barrier((sums, made, acts))
    blocks = exchange(sums.reshape(count, 2 * share, width), chips)
    final = jnp.sum(blocks.astype(f32), axis=0).astype(bf16)

    made_far = other_core(made[:, units:])
    made_far, waiting = lax.optimization_barrier((made_far, acts))
    acts_far = other_core(waiting)
    grad_weight_in, grad_weight_out = whole(
        bind(weight_kernel, xs, rows),
        "weight_gradients",
        (shaped(width, units), shaped(units, width)),
        (acts, acts_far, made[:, :units], made_far),
        4 * held * width * units,
    )
    return final[:share], final[share:], grad_weight_in, grad_weight_out


def solution(mesh):
    sizes = dict(mesh.shape)
    finer = Mesh(
        mesh.devices.reshape(sizes["row"], sizes["col"], sizes["depth"] // 2, 2),
        ("row", "col", "x", "core"),
    )
    wide = ("col", "x", "core")
    placed = (P(wide, "row"), P("row", wide), P(wide, "row"), P(wide, "row"))
    return jax.shard_map(
        local,
        mesh=finer,
        in_specs=placed,
        out_specs=(P(wide, "row"), P(wide, "row"), P("row", wide), P(wide, "row")),
        check_vma=False,
    )
```

```python
import math

import jax
import jax.numpy as jnp
from jax import lax
from jax.experimental import pallas as pl
from jax.experimental.pallas import tpu as pltpu
from jax.sharding import Mesh, PartitionSpec as P

root_two_pi = math.sqrt(2.0 / math.pi)
cubic = 0.044715
chips = ("x", "col")
bf16 = jnp.bfloat16
f32 = jnp.float32
mib = 1024 * 1024
swap_cover = 24_000_000_000


def gelu_parts(hidden):
    inner = jnp.tanh(root_two_pi * (hidden + cubic * hidden * hidden * hidden))
    value = 0.5 * hidden * (1.0 + inner)
    slope = 0.5 * (1.0 + inner) + 0.5 * hidden * (1.0 - inner * inner) * root_two_pi * (
        1.0 + 3.0 * cubic * hidden * hidden
    )
    return value, slope


def contract(left, right, left_dim, right_dim):
    return lax.dot_general(
        left, right, (((left_dim,), (right_dim,)), ((), ())), preferred_element_type=f32
    )


def other_core(block):
    return lax.ppermute(block, "core", [(0, 1), (1, 0)])


def exchange(blocks, axes):
    return lax.all_to_all(blocks, axes, split_axis=0, concat_axis=0)


def whole(kernel, name, out_shapes, args, flops, out_specs=None, scratch=(), limit=24):
    moved = sum(2 * math.prod(a.shape) for a in (*args, *jax.tree.leaves(out_shapes)))
    in_vmem = pl.BlockSpec(memory_space=pltpu.VMEM)
    return pl.pallas_call(
        kernel,
        out_shape=out_shapes,
        in_specs=[in_vmem] * len(args),
        out_specs=out_specs or jax.tree.map(lambda _: in_vmem, out_shapes),
        scratch_shapes=list(scratch),
        cost_estimate=pl.CostEstimate(flops=flops, bytes_accessed=moved, transcendentals=0),
        compiler_params=pltpu.CompilerParams(vmem_limit_bytes=limit * mib),
        name=name,
    )(*args)


def pairs_of(rows, group):
    pairs = rows.reshape(rows.shape[0] // (2 * group), 2, group, rows.shape[1])
    return pairs[:, 0], pairs[:, 1]


def meet(upper, lower, group):
    first = lax.broadcasted_iota(jnp.int32, upper.shape, 1) < group // 2
    return jnp.where(first, upper, lower)


def turned(groups):
    return pltpu.roll(groups, groups.shape[1] // 2, 1)


def kinds_of(ref, blocks, columns=slice(None)):
    size = ref.shape[0] // blocks
    return [
        jnp.concatenate(
            [
                ref[block * size + kind * size // 2 : block * size + (kind + 1) * size // 2, columns]
                for block in range(blocks)
            ],
            axis=0,
        )
        for kind in range(2)
    ]


def spread_kernel(share, line_ref, out_ref):
    group = 2 * share
    even, odd = pairs_of(line_ref[...].astype(f32), group)
    half = out_ref.shape[1] // 2
    tokens = meet(even, turned(odd), group).reshape(half, -1).astype(bf16)
    cotangent = meet(turned(even), odd, group).reshape(half, -1).astype(bf16)
    for place in range(out_ref.shape[0]):
        out_ref[place, :half] = tokens
        out_ref[place, half:] = cotangent


def terms_kernel(lines, rows, acts_ref, in_ref, out_ref, in_far_ref, out_far_ref, terms_ref):
    tokens, cotangent = kinds_of(acts_ref, lines)
    units = in_ref.shape[1]
    size = terms_ref.shape[0] // rows
    half = size // 2
    for place, (w_in, w_out) in enumerate(((in_ref, out_ref), (in_far_ref, out_far_ref))):
        columns = slice(place * units, (place + 1) * units)
        made = (contract(tokens, w_in[...], 1, 0), contract(cotangent, w_out[...], 1, 1))
        for kind, term in enumerate(made):
            term = term.astype(bf16)
            for row in range(rows):
                start = row * size + kind * half
                terms_ref[start : start + half, columns] = term[row * half : (row + 1) * half]


def gelu_kernel(terms_ref, out_ref):
    total = terms_ref[0].astype(f32)
    for row in range(1, terms_ref.shape[0]):
        total = total + terms_ref[row].astype(f32)
    half = total.shape[0] // 2
    value, slope = gelu_parts(total[:half])
    made = jnp.concatenate([value, total[half:] * slope], axis=0).astype(bf16)
    for row in range(out_ref.shape[0]):
        out_ref[row] = made


def sums_kernel(
    share, rows, made_ref, in_ref, out_ref, in_far_ref, out_far_ref, sums_hbm, sums_ref, sems
):
    units, width = out_ref.shape
    active, grads = kinds_of(made_ref, rows)
    group = 2 * share
    step = 512
    stores = []
    for place, start in enumerate(range(0, width, step)):
        part = slice(start, start + step)
        ahead = contract(active[:, :units], out_ref[:, part], 1, 0)
        ahead = ahead + contract(active[:, units:], out_far_ref[:, part], 1, 0)
        back = contract(grads[:, :units], in_ref[part, :], 1, 1)
        back = back + contract(grads[:, units:], in_far_ref[part, :], 1, 1)
        ahead, back = (sums.reshape(-1, group, step) for sums in (ahead, back))
        even, odd = meet(ahead, turned(back), group), meet(turned(ahead), back, group)
        picked = jnp.stack([even, odd], axis=1).reshape(-1, step)
        sums_ref[:, part] = picked.astype(bf16)
        store = pltpu.make_async_copy(
            sums_ref.at[:, part], sums_hbm.at[:, part], sems.at[place]
        )
        store.start()
        stores.append(store)
    for store in stores:
        store.wait()


def weight_kernel(
    lines, rows, acts_ref, acts_far_ref, made_ref, made_far_ref, grad_in_ref, grad_out_ref
):
    made = zip(kinds_of(made_ref, rows), kinds_of(made_far_ref, rows))
    active, grads = (jnp.concatenate(sides, axis=0) for sides in made)
    active = active.astype(f32).T.astype(bf16)
    step = 512
    for start in range(0, acts_ref.shape[1], step):
        part = slice(start, start + step)
        acts = zip(kinds_of(acts_ref, lines, part), kinds_of(acts_far_ref, lines, part))
        tokens, cotangent = (jnp.concatenate(sides, axis=0) for sides in acts)
        grad_in_ref[part, :] = contract(tokens, grads, 0, 0).astype(bf16)
        grad_out_ref[:, part] = contract(active, cotangent, 1, 0).astype(bf16)


def bind(kernel, *sizes):
    return lambda *refs: kernel(*sizes, *refs)


def local(tokens, weight_in, weight_out, cotangent):
    rows = lax.axis_size("row")
    count = lax.axis_size("col") * lax.axis_size("x")
    share, width = tokens.shape
    units = weight_in.shape[1]
    held = 2 * share * count
    shaped = lambda *dims: jax.ShapeDtypeStruct(dims, bf16)

    both = jnp.concatenate([tokens, cotangent], axis=0)
    weight_in_far = other_core(weight_in)
    weight_in_far, waiting = lax.optimization_barrier((weight_in_far, weight_out))
    weight_out_far = other_core(waiting)
    weights = (weight_in, weight_out, weight_in_far, weight_out_far)
    cols, xs = lax.axis_size("col"), lax.axis_size("x")
    line = exchange(jnp.broadcast_to(both[None], (cols,) + both.shape), "col")
    line = line.reshape(held // xs, width)
    line = whole(
        bind(spread_kernel, share), "spread_rows", shaped(xs, *line.shape), (line,), swap_cover
    )
    acts = exchange(line, "x").reshape(held, width)

    partial = whole(
        bind(terms_kernel, xs, rows),
        "hidden_terms",
        shaped(held, 2 * units),
        (acts, *weights),
        4 * held * width * units,
    )
    received = exchange(partial.reshape(rows, held // rows, 2 * units), "row")
    made = whole(
        gelu_kernel, "gelu_rows", shaped(*received.shape), (received,), 0
    )
    made = exchange(made, "row").reshape(held, 2 * units)

    sums = whole(
        bind(sums_kernel, share, rows),
        "output_terms",
        pltpu.HBM((held, width), bf16),
        (made, *weights),
        4 * held * width * units,
        out_specs=pl.BlockSpec(memory_space=pltpu.HBM),
        scratch=(pltpu.VMEM((held, width), bf16), pltpu.SemaphoreType.DMA((width // 512,))),
    )
    sums, made, acts = lax.optimization_barrier((sums, made, acts))
    blocks = exchange(sums.reshape(count, 2 * share, width), chips)
    final = jnp.sum(blocks.astype(f32), axis=0).astype(bf16)

    made_far = other_core(made[:, units:])
    made_far, held_acts = lax.optimization_barrier((made_far, acts))
    acts_far = other_core(held_acts)
    grad_weight_in, grad_weight_out = whole(
        bind(weight_kernel, xs, rows),
        "weight_gradients",
        (shaped(width, units), shaped(units, width)),
        (acts, acts_far, made[:, :units], made_far),
        4 * held * width * units,
    )
    return final[:share], final[share:], grad_weight_in, grad_weight_out


def solution(mesh):
    sizes = dict(mesh.shape)
    finer = Mesh(
        mesh.devices.reshape(sizes["row"], sizes["col"], sizes["depth"] // 2, 2),
        ("row", "col", "x", "core"),
    )
    wide = ("col", "x", "core")
    placed = (P(wide, "row"), P("row", wide), P(wide, "row"), P(wide, "row"))
    return jax.shard_map(
        local,
        mesh=finer,
        in_specs=placed,
        out_specs=(P(wide, "row"), P(wide, "row"), P("row", wide), P(wide, "row")),
        check_vma=False,
    )
```
